256 devices in a mesh: video: 32 (over z, x), audio: 8 (over y, core).
Axes of the slice: x: 4, y: 4, z: 8, core: 2. Of those that a mesh axis runs over, the one named last changes fastest.
Arguments:
- video_query: bfloat16 [16384, 3072], P('video', 'audio'), as said below
- video_kv: bfloat16 [2, 16384, 3072], P(None, 'video', 'audio'), may hold values from -6 to 6
- audio_qkv: bfloat16 [3, 2048, 3072], P(None, 'audio')
- video_count: int32 [64], P('video'), may hold values from 64 to 256, as said below
- audio_count: int32 [32], replicated, may hold values from 16 to 64, as said below
- video_range: int32 [32, 2], replicated, may hold values from 0 to 64, as said below
Outputs:
- video_out: bfloat16 [16384, 3072], P('video', 'audio')
- audio_out: bfloat16 [2048, 3072], P(None, 'audio')
The draws below stay inside these ranges and needn't reach their ends.
Inputs may be any that keep to these rules, and one draw needn't show every extreme that they name: `video_query`: queries. `video_count`: some video block is full. `audio_count`: some audio block is full. `video_range`: audio block i meets video blocks i * 2 to (i + 1) * 2 - 1 and possibly more, all within (i - 2) * 2 to (i + 3) * 2 - 1; start before end.
All inputs are finite; a program needn't handle non-finite values.
Results may differ from the reference program's by a relative error of at most 0.0045.
Values may be sent and summed in bfloat16 or wider, within the bound.
No kernel may reach another device: no remote copies, remote signals or barrier semaphores. Data moves between devices by JAX's collectives and lax.ppermute only.
A program may use at most 256 MiB of HBM per device.

```python
import math
import jax
import jax.numpy as jnp
from jax import lax

D = 3072
HEADS = 24
VBS = 256
ABS = 64
REACH = 2
VBLK = 2
ABLK = 4
VTOK = 16384
ATOK = 2048
NVB = 64
NAB = 32
RATIO = 2
N_VIDEO = 32
N_AUDIO = 8


def draw_video_query(key, part):
    key = jax.random.fold_in(key, 31)
    base_key = jax.random.fold_in(key, 0)
    values = jnp.clip(jax.random.normal(base_key, (VTOK, D), jnp.float32), -6.0, 6.0)
    return values.astype(jnp.bfloat16)


def draw_audio_qkv(key, part):
    key = jax.random.fold_in(key, 37)
    base_key = jax.random.fold_in(key, 0)
    values = jnp.clip(jax.random.normal(base_key, (3, ATOK, D), jnp.float32), -6.0, 6.0)
    return values.astype(jnp.bfloat16)


def draw_video_count(key, part):
    key = jax.random.fold_in(key, 41)
    count_key, full_key, least_key = jax.random.split(key, 3)
    counts = jax.random.randint(count_key, (NVB,), VBS // 4, VBS + 1)
    positions = jnp.arange(NVB, dtype=jnp.int32)
    full_spot = jax.random.randint(full_key, (), 0, NVB)
    least_spot = (full_spot + 1 + jax.random.randint(least_key, (), 0, NVB - 1)) % NVB
    counts = jnp.where(positions == full_spot, VBS, counts)
    counts = jnp.where(positions == least_spot, VBS // 4, counts)
    return counts.astype(jnp.int32)


def draw_audio_count(key, part):
    key = jax.random.fold_in(key, 43)
    count_key, full_key, least_key = jax.random.split(key, 3)
    counts = jax.random.randint(count_key, (NAB,), ABS // 4, ABS + 1)
    positions = jnp.arange(NAB, dtype=jnp.int32)
    full_spot = jax.random.randint(full_key, (), 0, NAB)
    least_spot = (full_spot + 1 + jax.random.randint(least_key, (), 0, NAB - 1)) % NAB
    counts = jnp.where(positions == full_spot, ABS, counts)
    counts = jnp.where(positions == least_spot, ABS // 4, counts)
    return counts.astype(jnp.int32)


def draw_video_range(key, part):
    key = jax.random.fold_in(key, 47)
    before_key, after_key = jax.random.split(key)
    positions = jnp.arange(NAB, dtype=jnp.int32)
    extent = REACH * VBLK
    before = jax.random.randint(before_key, (NAB,), 0, extent + 1)
    after = jax.random.randint(after_key, (NAB,), 0, extent + 1)
    middle = NAB // 2
    before = jnp.where(positions == middle, extent, before)
    after = jnp.where(positions == middle, extent, after)
    range_start = jnp.maximum(positions * RATIO - before, 0)
    range_end = jnp.minimum((positions + 1) * RATIO + after, NVB)
    return jnp.stack([range_start, range_end], axis=1).astype(jnp.int32)


def block_levels(rng, dims, shards, low, top_value):
    def one(position, parts):
        draws = jax.random.uniform(jax.random.fold_in(jax.random.fold_in(rng, 6), position), (parts,), jnp.float32, low / len(shards), top_value / len(shards))
        return jnp.repeat(jnp.exp(draws), dims[position] // parts).reshape((-1,) + (1,) * (len(dims) - position - 1))

    level = one(*shards[0])
    for cut in shards[1:]:
        level = level * one(*cut)
    return level


def noise(rng, dims, width, reach, cuts=(), held_as=jnp.bfloat16):
    result = jax.random.normal(rng, dims, jnp.float32) * width
    if len(cuts) > 0:
        result = block_levels(rng, dims, cuts, -0.22, 0.18) * result
    return jnp.clip(result, min=-reach, max=reach).astype(held_as)


def setup_inputs(seed: int = 0) -> dict:
    keys = jax.random.split(jax.random.key(seed), 7)
    video_query = draw_video_query(jax.random.fold_in(keys[6], 71), 0)
    video_kv = noise(keys[1], (2, VTOK, D), 1.0, 6.0, ((1, 32), (2, 8)))
    audio_qkv = draw_audio_qkv(jax.random.fold_in(keys[6], 71), 0)
    video_count = draw_video_count(jax.random.fold_in(keys[6], 71), 0)
    audio_count = draw_audio_count(jax.random.fold_in(keys[6], 71), 0)
    video_range = draw_video_range(jax.random.fold_in(keys[6], 71), 0)
    return dict(video_query=video_query, video_kv=video_kv, audio_qkv=audio_qkv, video_count=video_count, audio_count=audio_count, video_range=video_range)


def pair_rules(segment_index, count_here, audio_count, video_range, period, seg_rows, win_rows):
    blocks_total = audio_count.shape[0]
    win_index = jnp.arange(win_rows, dtype=jnp.int32)
    audio_block = segment_index * period - REACH * period + win_index // ABS
    inside = (audio_block >= 0) & (audio_block < blocks_total)
    matches = audio_block[:, None] == jnp.arange(blocks_total, dtype=jnp.int32)[None, :]
    range_start = lax.optimization_barrier(jnp.sum(jnp.where(matches, video_range[None, :, 0], 0), axis=1))
    range_end = lax.optimization_barrier(jnp.sum(jnp.where(matches, video_range[None, :, 1], 0), axis=1))
    live_count = lax.optimization_barrier(jnp.sum(jnp.where(matches, audio_count[None, :], 0), axis=1))
    audio_live = inside & (win_index % ABS < live_count)
    tok_index = jnp.arange(seg_rows, dtype=jnp.int32)
    video_block = segment_index * (seg_rows // VBS) + tok_index // VBS
    video_live = tok_index % VBS < jnp.repeat(count_here, VBS)
    paired = inside[:, None] & (range_start[:, None] <= video_block[None, :]) & (video_block[None, :] < range_end[:, None])
    return (paired, audio_live, video_live)

def soft_parts(scores, allowed):
    masked = jnp.where(allowed, scores, -1e+30)
    row_peak = lax.optimization_barrier(jnp.max(masked, axis=-1, keepdims=True))
    raised = jnp.where(allowed, jnp.exp(scores - row_peak), 0.0)
    return (row_peak[..., 0], lax.optimization_barrier(jnp.sum(raised, axis=-1)), raised.astype(jnp.bfloat16))

def merge_parts(former, latter):
    row_peak = jnp.maximum(former[0], latter[0])
    keep_former = jnp.exp(former[0] - row_peak)
    keep_latter = jnp.exp(latter[0] - row_peak)
    row_total = former[1] * keep_former + latter[1] * keep_latter
    per_head = former[2].shape[1] // row_peak.shape[0]
    blended = former[2] * jnp.repeat(keep_former.T, per_head, axis=1) + latter[2] * jnp.repeat(keep_latter.T, per_head, axis=1)
    return (row_peak, row_total, blended)

def reference(video_query, video_kv, audio_qkv, video_count, audio_count, video_range):
    head_dim = D // HEADS
    period = ABLK * N_AUDIO // N_VIDEO
    span_rows = period * ABS
    lead_rows = REACH * span_rows
    win_rows = (2 * REACH + 1) * span_rows
    seg_rows = VBLK * VBS
    audio_total = audio_qkv.shape[1]
    score_scale = 1.0 / math.sqrt(head_dim)
    padding = jnp.zeros((3, lead_rows, D), audio_qkv.dtype)
    padded = jnp.concatenate([padding, audio_qkv, padding], axis=1)

    def segment(running, segment_index):
        window = lax.dynamic_slice_in_dim(padded, segment_index * span_rows, win_rows, 1)
        video_pair = lax.dynamic_slice_in_dim(video_kv, segment_index * seg_rows, seg_rows, 1)
        queries = lax.dynamic_slice_in_dim(video_query, segment_index * seg_rows, seg_rows, 0)
        count_here = lax.dynamic_slice_in_dim(video_count, segment_index * VBLK, VBLK, 0)
        paired, audio_live, video_live = pair_rules(segment_index, count_here, audio_count, video_range, period, seg_rows, win_rows)
        queries = queries.astype(jnp.float32).reshape(seg_rows, HEADS, head_dim)
        audio_keys = window[1].astype(jnp.float32).reshape(win_rows, HEADS, head_dim)
        audio_values = window[2].astype(jnp.float32).reshape(win_rows, HEADS, head_dim)
        scores = jnp.einsum('thd,rhd->htr', queries, audio_keys) * score_scale
        row_peak, row_total, weights = soft_parts(scores, (paired.T & audio_live[None, :])[None])
        weights = lax.optimization_barrier(weights).astype(jnp.float32)
        blended = jnp.einsum('htr,rhd->thd', weights, audio_values) / row_total.T[:, :, None]
        video_part = blended.reshape(seg_rows, D).astype(jnp.bfloat16)
        audio_queries = window[0].astype(jnp.float32).reshape(win_rows, HEADS, head_dim)
        video_keys = video_pair[0].astype(jnp.float32).reshape(seg_rows, HEADS, head_dim)
        video_values = video_pair[1].astype(jnp.float32).reshape(seg_rows, HEADS, head_dim)
        scores_back = jnp.einsum('rhd,thd->hrt', audio_queries, video_keys) * score_scale
        part_peak, part_total, part_weights = soft_parts(scores_back, (paired & video_live[None, :])[None])
        part_weights = lax.optimization_barrier(part_weights).astype(jnp.float32)
        part_out = jnp.einsum('hrt,thd->rhd', part_weights, video_values).reshape(win_rows, D)
        big_peak, big_total, big_out = running
        start_row = segment_index * span_rows
        former = (lax.dynamic_slice_in_dim(big_peak, start_row, win_rows, 1), lax.dynamic_slice_in_dim(big_total, start_row, win_rows, 1), lax.dynamic_slice_in_dim(big_out, start_row, win_rows, 0))
        joined = merge_parts(former, (part_peak, part_total, part_out))
        running = (lax.dynamic_update_slice_in_dim(big_peak, joined[0], start_row, 1), lax.dynamic_update_slice_in_dim(big_total, joined[1], start_row, 1), lax.dynamic_update_slice_in_dim(big_out, joined[2], start_row, 0))
        return (running, video_part)
    padded_rows = audio_total + 2 * lead_rows
    initial = (jnp.full((HEADS, padded_rows), -1e+30, jnp.float32), jnp.zeros((HEADS, padded_rows), jnp.float32), jnp.zeros((padded_rows, D), jnp.float32))
    running, video_parts = lax.scan(segment, initial, jnp.arange(N_VIDEO, dtype=jnp.int32))
    video_out = video_parts.reshape(N_VIDEO * seg_rows, D)
    final_total = running[1][:, lead_rows:lead_rows + audio_total]
    final_out = running[2][lead_rows:lead_rows + audio_total]
    audio_out = (final_out / jnp.repeat(final_total.T, head_dim, axis=1)).astype(jnp.bfloat16)
    return (video_out, audio_out)
```

```python
import math

import jax
import jax.numpy as jnp
from jax import lax
from jax.experimental import pallas as pl
from jax.experimental.pallas import tpu as pltpu
from jax.sharding import PartitionSpec as P

HEADS = 24
VBS = 256
ABS = 64
REACH = 2
ZS = 8
XS = 4
NEG = -1e30
LOG2E = 1.4426950408889634
BOTH = ("video", "audio")

VMEM = pl.BlockSpec(memory_space=pltpu.VMEM)
SMEM = pl.BlockSpec(memory_space=pltpu.SMEM)
ANY = pl.BlockSpec(memory_space=pl.ANY)


def params():
    return pltpu.CompilerParams(vmem_limit_bytes=24 * 1024 * 1024)


def place():
    v = lax.axis_index("video")
    return v, v // XS, v % XS


def pack_kernel(src, q_own, q_out, kv_own, kv_out, sems):
    _, z, x = place()
    columns = q_own.shape[1]
    cols = pl.ds(pl.multiple_of(z * columns, 128), columns)
    half = q_out.shape[0]
    rows = pl.ds(pl.multiple_of(jnp.where(x < REACH, half, 0), half), half)
    copies = [
        pltpu.make_async_copy(src.at[0, :, cols], q_own, sems.at[0]),
        pltpu.make_async_copy(src.at[0, rows, cols], q_out, sems.at[1]),
        pltpu.make_async_copy(src.at[pl.ds(1, 2), :, cols], kv_own, sems.at[2]),
        pltpu.make_async_copy(src.at[pl.ds(1, 2), rows, cols], kv_out, sems.at[3]),
    ]
    for c in copies:
        c.start()
    for c in copies:
        c.wait()


def split3(value):
    hi = value.astype(jnp.bfloat16).astype(jnp.float32)
    rest = value - hi
    mid = rest.astype(jnp.bfloat16).astype(jnp.float32)
    return hi, mid, rest - mid


def audio_kernel(scale, count, ranges, q_own, q_out, kv, *refs):
    outs, (queries, bias) = refs[:5], refs[5:]
    v, z, x = place()
    blocks = ranges.shape[0]
    columns = q_own.shape[1]
    heads = columns // 128
    lane = lax.broadcasted_iota(jnp.int32, (ABS, 2 * VBS), 1)
    for slot in range(5):
        offset = slot - REACH
        at = x + offset
        dst = pl.ds(slot * ABS, ABS)
        own = (at >= 0) & (at < XS)

        @pl.when(own)
        def _():
            queries[dst, :] = q_own[pl.ds(pl.multiple_of(at * ABS, ABS), ABS), :]

        @pl.when(jnp.logical_not(own))
        def _():
            row = jnp.where(at < 0, at + REACH, at - XS) * ABS
            queries[dst, :] = q_out[pl.ds(pl.multiple_of(row, ABS), ABS), :]

        block = v + offset
        inside = (block >= 0) & (block < blocks)
        safe = jnp.clip(block, 0, blocks - 1)
        first, last = ranges[safe, 0], ranges[safe, 1]
        live = []
        for j in range(2):
            vb = v * 2 + j
            paired = inside & (first <= vb) & (vb < last)
            live.append(jnp.where(paired, count[j], 0))
        allowed = (lane < live[0]) | ((lane >= VBS) & (lane < VBS + live[1]))
        bias[dst, :] = jnp.where(allowed, 0.0, NEG)
    stat_lane = lax.broadcasted_iota(jnp.int32, (5 * ABS, 128), 1)
    stats = jnp.zeros((5 * ABS, 128), jnp.float32)
    for h in range(heads):
        cols = slice(h * 128, (h + 1) * 128)
        s = lax.dot_general(
            queries[:, cols], kv[0, :, cols], (((1,), (1,)), ((), ())),
            preferred_element_type=jnp.float32,
        )
        s = s + bias[...]
        peak = jnp.max(s, axis=1, keepdims=True)
        e = jnp.exp2((s - peak) * scale)
        total = jnp.sum(e, axis=1, keepdims=True)
        o = lax.dot_general(
            e.astype(jnp.bfloat16), kv[1, :, cols], (((1,), (0,)), ((), ())),
            preferred_element_type=jnp.float32,
        )
        for i, part in enumerate(split3(peak * scale) + split3(total)):
            stats = jnp.where(stat_lane == h * 6 + i, part, stats)
        for slot in range(5):
            outs[slot][:, cols] = o[slot * ABS : (slot + 1) * ABS].astype(jnp.bfloat16)
    for slot in range(5):
        outs[slot][:, columns:] = stats[slot * ABS : (slot + 1) * ABS].astype(jnp.bfloat16)


def merge_kernel(*refs):
    parts, out = refs[:-1], refs[-1]
    columns = out.shape[1]
    stats = [p[:, columns:].astype(jnp.float32) for p in parts]
    for h in range(columns // 128):
        cols = slice(h * 128, (h + 1) * 128)

        def stat(s, i):
            at = h * 6 + i
            return s[:, at : at + 1] + s[:, at + 1 : at + 2] + s[:, at + 2 : at + 3]

        peaks = [stat(s, 0) for s in stats]
        peak = peaks[0]
        for p in peaks[1:]:
            peak = jnp.maximum(peak, p)
        total, blend = 0.0, 0.0
        for s, p, part in zip(stats, peaks, parts):
            keep = jnp.exp2(p - peak)
            total = total + stat(s, 3) * keep
            blend = blend + part[:, cols].astype(jnp.float32) * keep
        out[:, cols] = (blend / total).astype(jnp.bfloat16)


def video_kernel(scale, audio_count, ranges, query, kv_own, kv_out, out, bias):
    v, z, x = place()
    blocks = ranges.shape[0]
    columns = query.shape[1]
    keys = kv_own.shape[1] + kv_out.shape[1]
    own_keys = kv_own.shape[1]
    lane = lax.broadcasted_iota(jnp.int32, (8, ABS * 2), 1)
    for pair in range(keys // (2 * ABS)):
        for j in range(2):
            vb = v * 2 + j
            allowed = None
            for side in range(2):
                pos = pair * 2 + side
                if pos < XS:
                    block = z * XS + pos
                else:
                    block = z * XS + (pos - XS) + jnp.where(x < REACH, -REACH, XS)
                inside = (block >= 0) & (block < blocks)
                safe = jnp.clip(block, 0, blocks - 1)
                paired = inside & (ranges[safe, 0] <= vb) & (vb < ranges[safe, 1])
                live = jnp.where(paired, audio_count[safe], 0)
                here = (lane >= side * ABS) & (lane < side * ABS + live)
                allowed = here if allowed is None else allowed | here
            bias[j, :, pair * 2 * ABS : (pair + 1) * 2 * ABS] = jnp.where(allowed, 0.0, NEG)
    for j in range(2):
        rows = slice(j * VBS, (j + 1) * VBS)
        for h in range(columns // 128):
            cols = slice(h * 128, (h + 1) * 128)
            dims = (((1,), (1,)), ((), ()))
            s1 = lax.dot_general(
                query[rows, cols], kv_own[0, :, cols], dims, preferred_element_type=jnp.float32
            )
            s2 = lax.dot_general(
                query[rows, cols], kv_out[0, :, cols], dims, preferred_element_type=jnp.float32
            )
            s1 = s1 + bias[j, 0:1, :own_keys]
            s2 = s2 + bias[j, 0:1, own_keys:]
            peak = jnp.maximum(
                jnp.max(s1, axis=1, keepdims=True), jnp.max(s2, axis=1, keepdims=True)
            )
            e1 = jnp.exp2((s1 - peak) * scale)
            e2 = jnp.exp2((s2 - peak) * scale)
            total = jnp.sum(e1, axis=1, keepdims=True) + jnp.sum(e2, axis=1, keepdims=True)
            dims = (((1,), (0,)), ((), ()))
            o = lax.dot_general(
                e1.astype(jnp.bfloat16), kv_own[1, :, cols], dims,
                preferred_element_type=jnp.float32,
            ) + lax.dot_general(
                e2.astype(jnp.bfloat16), kv_out[1, :, cols], dims,
                preferred_element_type=jnp.float32,
            )
            out[rows, cols] = (o / total).astype(jnp.bfloat16)


ZHELD = (0, 3, -2, 1, -1, 4, 2, -3)


def assemble_kernel(*refs):
    chunks, out, sems = refs[:8], refs[8], refs[9]
    _, z, x = place()
    copies = []
    for i, rel in enumerate(ZHELD):
        zz = lax.rem(z + rel + ZS, ZS)
        for k in range(XS):
            row = (zz * XS + lax.rem(x - k + XS, XS)) * ABS
            copies.append(
                pltpu.make_async_copy(
                    chunks[i].at[pl.ds(k * ABS, ABS), :],
                    out.at[pl.ds(pl.multiple_of(row, ABS), ABS), :],
                    sems.at[i * XS + k],
                )
            )
    for c in copies:
        c.start()
    for c in copies:
        c.wait()


def shifted(value, step):
    n = ZS * XS
    return lax.ppermute(value, "video", [(v, (v + step) % n) for v in range(n)])


def along_x(value, step):
    pairs = [(z * XS + x, z * XS + (x + step) % XS) for z in range(ZS) for x in range(XS)]
    return lax.ppermute(value, "video", pairs)


def from_z(value, rel):
    return shifted(value, -rel * XS)


def local(video_query, video_kv, audio_qkv, video_count, audio_count, video_range):
    seg_rows, columns = video_query.shape
    shard_rows = audio_qkv.shape[1]
    half = REACH * ABS
    bf16 = jnp.bfloat16
    f32 = jnp.float32
    scale = LOG2E / math.sqrt(128)
    audio_devices = lax.axis_size("audio")

    def flat(z, x, a):
        return ((z % ZS) * XS + x) * audio_devices + a

    q_own, q_out, kv_own, kv_out = pl.pallas_call(
        pack_kernel,
        out_shape=(
            jax.ShapeDtypeStruct((shard_rows, columns), bf16),
            jax.ShapeDtypeStruct((half, columns), bf16),
            jax.ShapeDtypeStruct((2, shard_rows, columns), bf16),
            jax.ShapeDtypeStruct((2, half, columns), bf16),
        ),
        in_specs=[ANY],
        out_specs=(VMEM,) * 4,
        scratch_shapes=[pltpu.SemaphoreType.DMA((4,))],
        compiler_params=params(),
        name="pack",
    )(audio_qkv)
    every = [(z, x, a) for z in range(ZS) for x in range(XS) for a in range(audio_devices)]
    own_pairs = [(flat(z, x, a), flat(a, x, z)) for z, x, a in every]
    out_pairs = [
        (flat(z, x, a), flat(a + 1 if x < REACH else a - 1, x, z)) for z, x, a in every
    ]
    q_own = lax.ppermute(q_own, BOTH, own_pairs)
    q_out = lax.ppermute(q_out, BOTH, out_pairs)
    kv_own = lax.ppermute(kv_own, BOTH, own_pairs)
    kv_out = lax.ppermute(kv_out, BOTH, out_pairs)

    packed = jax.ShapeDtypeStruct((ABS, columns + 128), bf16)
    parts = pl.pallas_call(
        lambda *refs: audio_kernel(scale, *refs),
        out_shape=(packed,) * 5,
        in_specs=[SMEM, SMEM, VMEM, VMEM, VMEM],
        out_specs=(VMEM,) * 5,
        scratch_shapes=[
            pltpu.VMEM((5 * ABS, columns), bf16),
            pltpu.VMEM((5 * ABS, seg_rows), f32),
        ],
        compiler_params=params(),
        name="audio_side",
    )(video_count, video_range, q_own, q_out, video_kv)
    held = [
        shifted(part, slot - REACH) if slot != REACH else part for slot, part in enumerate(parts)
    ]
    block_out = pl.pallas_call(
        merge_kernel,
        out_shape=jax.ShapeDtypeStruct((ABS, columns), bf16),
        in_specs=[VMEM] * 5,
        out_specs=VMEM,
        compiler_params=params(),
        name="merge",
    )(*held)

    video_out = pl.pallas_call(
        lambda *refs: video_kernel(scale, *refs),
        out_shape=jax.ShapeDtypeStruct((seg_rows, columns), bf16),
        in_specs=[SMEM, SMEM, VMEM, VMEM, VMEM],
        out_specs=VMEM,
        scratch_shapes=[pltpu.VMEM((2, 8, shard_rows + half), f32)],
        compiler_params=params(),
        name="video_side",
    )(audio_count, video_range, video_query, kv_own, kv_out)

    row = jnp.concatenate([block_out] + [along_x(block_out, k) for k in range(1, XS)], axis=0)
    z3, zm2 = from_z(row, 3), from_z(row, -2)
    z1, zm1 = from_z(row, 1), from_z(row, -1)
    z4, z2, zm3 = from_z(z3, 1), from_z(z3, -1), from_z(zm2, -1)
    audio_out = pl.pallas_call(
        assemble_kernel,
        out_shape=jax.ShapeDtypeStruct((ZS * XS * ABS, columns), bf16),
        in_specs=[VMEM] * 8,
        out_specs=ANY,
        scratch_shapes=[pltpu.SemaphoreType.DMA((ZS * XS,))],
        compiler_params=params(),
        name="assemble",
    )(row, z3, zm2, z1, zm1, z4, z2, zm3)
    return (video_out, audio_out)


def solution(mesh):
    return jax.shard_map(
        local,
        mesh=mesh,
        in_specs=(
            P("video", "audio"),
            P(None, "video", "audio"),
            P(None, "audio", None),
            P("video"),
            P(),
            P(),
        ),
        out_specs=(P("video", "audio"), P(None, "audio")),
        check_vma=False,
    )
```

```python
import math

import jax
import jax.numpy as jnp
from jax import lax
from jax.experimental import pallas as pl
from jax.experimental.pallas import tpu as pltpu
from jax.sharding import PartitionSpec as P

HEADS = 24
VBS = 256
ABS = 64
REACH = 2
ZS = 8
XS = 4
NEG = -1e30
LOG2E = 1.4426950408889634
BOTH = ("video", "audio")

VMEM = pl.BlockSpec(memory_space=pltpu.VMEM)
SMEM = pl.BlockSpec(memory_space=pltpu.SMEM)
ANY = pl.BlockSpec(memory_space=pl.ANY)


def params():
    return pltpu.CompilerParams(vmem_limit_bytes=24 * 1024 * 1024)


def place():
    v = lax.axis_index("video")
    return v, v // XS, v % XS


def sender_row(z, shard):
    ahead = lax.rem(z - shard + ZS, ZS)
    turn = jnp.where(ahead == 0, 2, jnp.where(ahead == 1, 1, jnp.where(ahead == ZS - 1, 3, 0)))
    return lax.rem(shard // 2 + turn, 4)


def line_of_sender(z, turn):
    return z + (2 if z % 2 else -2, 1, 0, -1)[turn]


def pack_kernel(first_part, parts, src, out0, out1, sems):
    _, z, _ = place()
    columns = out0.shape[-1]
    first = sender_row(z, lax.axis_index("audio")) * 2 * columns
    copies = []
    for core, out in enumerate((out0, out1)):
        cols = pl.ds(pl.multiple_of(first + core * columns, 128), columns)
        for i in range(parts):
            copies.append(
                pltpu.make_async_copy(
                    src.at[first_part + i, :, cols], out.at[i], sems.at[core * parts + i]
                )
            )
    for c in copies:
        c.start()
    for c in copies:
        c.wait()


def split3(value):
    hi = value.astype(jnp.bfloat16).astype(jnp.float32)
    rest = value - hi
    mid = rest.astype(jnp.bfloat16).astype(jnp.float32)
    return hi, mid, rest - mid


def audio_kernel(scale, count, ranges, q_own, q_out, kv, *refs):
    outs, (queries, bias) = refs[:5], refs[5:]
    v, z, x = place()
    blocks = ranges.shape[0]
    columns = q_own.shape[1]
    heads = columns // 128
    lane = lax.broadcasted_iota(jnp.int32, (ABS, 2 * VBS), 1)
    for slot in range(5):
        offset = slot - REACH
        at = x + offset
        dst = pl.ds(slot * ABS, ABS)
        own = (at >= 0) & (at < XS)

        @pl.when(own)
        def _():
            queries[dst, :] = q_own[pl.ds(pl.multiple_of(at * ABS, ABS), ABS), :]

        @pl.when(jnp.logical_not(own))
        def _():
            row = jnp.where(at < 0, at + REACH, at - XS) * ABS
            queries[dst, :] = q_out[pl.ds(pl.multiple_of(row, ABS), ABS), :]

        block = v + offset
        inside = (block >= 0) & (block < blocks)
        safe = jnp.clip(block, 0, blocks - 1)
        first, last = ranges[safe, 0], ranges[safe, 1]
        live = []
        for j in range(2):
            vb = v * 2 + j
            paired = inside & (first <= vb) & (vb < last)
            live.append(jnp.where(paired, count[j], 0))
        allowed = (lane < live[0]) | ((lane >= VBS) & (lane < VBS + live[1]))
        bias[dst, :] = jnp.where(allowed, 0.0, NEG)
    stat_lane = lax.broadcasted_iota(jnp.int32, (5 * ABS, 128), 1)
    stats = jnp.zeros((5 * ABS, 128), jnp.float32)
    for h in range(heads):
        cols = slice(h * 128, (h + 1) * 128)
        s = lax.dot_general(
            queries[:, cols], kv[0, :, cols], (((1,), (1,)), ((), ())),
            preferred_element_type=jnp.float32,
        )
        s = s + bias[...]
        peak = jnp.max(s, axis=1, keepdims=True)
        e = jnp.exp2((s - peak) * scale)
        total = jnp.sum(e, axis=1, keepdims=True)
        o = lax.dot_general(
            e.astype(jnp.bfloat16), kv[1, :, cols], (((1,), (0,)), ((), ())),
            preferred_element_type=jnp.float32,
        )
        for i, part in enumerate(split3(peak * scale) + split3(total)):
            stats = jnp.where(stat_lane == h * 6 + i, part, stats)
        for slot in range(5):
            outs[slot][:, cols] = o[slot * ABS : (slot + 1) * ABS].astype(jnp.bfloat16)
    for slot in range(5):
        outs[slot][:, columns:] = stats[slot * ABS : (slot + 1) * ABS].astype(jnp.bfloat16)


def merge_kernel(*refs):
    parts, out = refs[:-1], refs[-1]
    columns = out.shape[1]
    stats = [p[:, columns:].astype(jnp.float32) for p in parts]
    for h in range(columns // 128):
        cols = slice(h * 128, (h + 1) * 128)

        def stat(s, i):
            at = h * 6 + i
            return s[:, at : at + 1] + s[:, at + 1 : at + 2] + s[:, at + 2 : at + 3]

        peaks = [stat(s, 0) for s in stats]
        peak = peaks[0]
        for p in peaks[1:]:
            peak = jnp.maximum(peak, p)
        total, blend = 0.0, 0.0
        for s, p, part in zip(stats, peaks, parts):
            keep = jnp.exp2(p - peak)
            total = total + stat(s, 3) * keep
            blend = blend + part[:, cols].astype(jnp.float32) * keep
        out[:, cols] = (blend / total).astype(jnp.bfloat16)


def video_kernel(scale, audio_count, ranges, query, kv_own, kv_out, out, bias):
    v, z, x = place()
    blocks = ranges.shape[0]
    columns = query.shape[1]
    keys = kv_own.shape[1] + kv_out.shape[1]
    own_keys = kv_own.shape[1]
    lane = lax.broadcasted_iota(jnp.int32, (8, ABS * 2), 1)
    for pair in range(keys // (2 * ABS)):
        for j in range(2):
            vb = v * 2 + j
            allowed = None
            for side in range(2):
                pos = pair * 2 + side
                if pos < XS:
                    block = z * XS + pos
                else:
                    block = z * XS + (pos - XS) + jnp.where(x < REACH, -REACH, XS)
                inside = (block >= 0) & (block < blocks)
                safe = jnp.clip(block, 0, blocks - 1)
                paired = inside & (ranges[safe, 0] <= vb) & (vb < ranges[safe, 1])
                live = jnp.where(paired, audio_count[safe], 0)
                here = (lane >= side * ABS) & (lane < side * ABS + live)
                allowed = here if allowed is None else allowed | here
            bias[j, :, pair * 2 * ABS : (pair + 1) * 2 * ABS] = jnp.where(allowed, 0.0, NEG)
    for j in range(2):
        rows = slice(j * VBS, (j + 1) * VBS)
        for h in range(columns // 128):
            cols = slice(h * 128, (h + 1) * 128)
            dims = (((1,), (1,)), ((), ()))
            s1 = lax.dot_general(
                query[rows, cols], kv_own[0, :, cols], dims, preferred_element_type=jnp.float32
            )
            s2 = lax.dot_general(
                query[rows, cols], kv_out[0, :, cols], dims, preferred_element_type=jnp.float32
            )
            s1 = s1 + bias[j, 0:1, :own_keys]
            s2 = s2 + bias[j, 0:1, own_keys:]
            peak = jnp.maximum(
                jnp.max(s1, axis=1, keepdims=True), jnp.max(s2, axis=1, keepdims=True)
            )
            e1 = jnp.exp2((s1 - peak) * scale)
            e2 = jnp.exp2((s2 - peak) * scale)
            total = jnp.sum(e1, axis=1, keepdims=True) + jnp.sum(e2, axis=1, keepdims=True)
            dims = (((1,), (0,)), ((), ()))
            o = lax.dot_general(
                e1.astype(jnp.bfloat16), kv_own[1, :, cols], dims,
                preferred_element_type=jnp.float32,
            ) + lax.dot_general(
                e2.astype(jnp.bfloat16), kv_out[1, :, cols], dims,
                preferred_element_type=jnp.float32,
            )
            out[rows, cols] = (o / total).astype(jnp.bfloat16)


ZHELD = (0, 3, -2, 1, -1, 4, 2, -3)


def assemble_kernel(*refs):
    chunks, out, sems = refs[:8], refs[8], refs[9]
    _, z, x = place()
    copies = []
    for i, rel in enumerate(ZHELD):
        zz = lax.rem(z + rel + ZS, ZS)
        for k in range(XS):
            row = (zz * XS + lax.rem(x - k + XS, XS)) * ABS
            copies.append(
                pltpu.make_async_copy(
                    chunks[i].at[pl.ds(k * ABS, ABS), :],
                    out.at[pl.ds(pl.multiple_of(row, ABS), ABS), :],
                    sems.at[i * XS + k],
                )
            )
    for c in copies:
        c.start()
    for c in copies:
        c.wait()


def shifted(value, step):
    n = ZS * XS
    return lax.ppermute(value, "video", [(v, (v + step) % n) for v in range(n)])


def along_x(value, step):
    pairs = [(z * XS + x, z * XS + (x + step) % XS) for z in range(ZS) for x in range(XS)]
    return lax.ppermute(value, "video", pairs)


def from_z(value, rel):
    return shifted(value, -rel * XS)


def local(video_query, video_kv, audio_qkv, video_count, audio_count, video_range):
    seg_rows, columns = video_query.shape
    shard_rows = audio_qkv.shape[1]
    half = REACH * ABS
    bf16 = jnp.bfloat16
    f32 = jnp.float32
    scale = LOG2E / math.sqrt(128)
    audio_devices = lax.axis_size("audio")

    def flat(z, x, a):
        return ((z % ZS) * XS + x) * audio_devices + a

    def packed_slices(first_part, parts, value, name):
        return pl.pallas_call(
            lambda *refs: pack_kernel(first_part, parts, *refs),
            out_shape=(jax.ShapeDtypeStruct((parts, shard_rows, columns), bf16),) * 2,
            in_specs=[ANY],
            out_specs=(VMEM,) * 2,
            scratch_shapes=[pltpu.SemaphoreType.DMA((2 * parts,))],
            compiler_params=pltpu.CompilerParams(vmem_limit_bytes=60 * 1024 * 1024),
            name=name,
        )(value)

    q0, q1 = packed_slices(0, 1, audio_qkv, "pack_queries")
    q0, q1, later = lax.optimization_barrier((q0, q1, audio_qkv))
    kv0, kv1 = packed_slices(1, 2, later, "pack_keys")
    x = lax.axis_index("video") % XS
    edge = jnp.where(x < REACH, half, 0)

    def to_core(value, core):
        pairs = []
        for z in range(ZS):
            for xx in range(XS):
                for y in range(audio_devices // 2):
                    sender = line_of_sender(z, (y - z // 2) % 4)
                    pairs.append((flat(sender, xx, z), flat(z, xx, 2 * y + core)))
        return lax.ppermute(value, BOTH, pairs)

    def from_next_line(value):
        n = ZS * XS
        pairs = [(v, (v + XS if v % XS < REACH else v - XS) % n) for v in range(n)]
        return lax.ppermute(value, "video", pairs)

    q_own = (to_core(q0, 0) + to_core(q1, 1))[0]
    q_out = from_next_line(lax.dynamic_slice_in_dim(q_own, edge, half, 0))
    kv0, kv1, q_own = lax.optimization_barrier((kv0, kv1, q_own))
    kv0, kv1 = to_core(kv0, 0), to_core(kv1, 1)

    packed = jax.ShapeDtypeStruct((ABS, columns + 128), bf16)
    parts = pl.pallas_call(
        lambda *refs: audio_kernel(scale, *refs),
        out_shape=(packed,) * 5,
        in_specs=[SMEM, SMEM, VMEM, VMEM, VMEM],
        out_specs=(VMEM,) * 5,
        scratch_shapes=[
            pltpu.VMEM((5 * ABS, columns), bf16),
            pltpu.VMEM((5 * ABS, seg_rows), f32),
        ],
        compiler_params=params(),
        name="audio_side",
    )(video_count, video_range, q_own, q_out, video_kv)
    held = [
        shifted(part, slot - REACH) if slot != REACH else part for slot, part in enumerate(parts)
    ]
    block_out = pl.pallas_call(
        merge_kernel,
        out_shape=jax.ShapeDtypeStruct((ABS, columns), bf16),
        in_specs=[VMEM] * 5,
        out_specs=VMEM,
        compiler_params=params(),
        name="merge",
    )(*held)

    row = jnp.concatenate([block_out] + [along_x(block_out, k) for k in range(1, XS)], axis=0)
    kv0, kv1, row = lax.optimization_barrier((kv0, kv1, row))
    kv_own = kv0 + kv1
    kv_out = from_next_line(lax.dynamic_slice_in_dim(kv_own, edge, half, 1))
    video_out = pl.pallas_call(
        lambda *refs: video_kernel(scale, *refs),
        out_shape=jax.ShapeDtypeStruct((seg_rows, columns), bf16),
        in_specs=[SMEM, SMEM, VMEM, VMEM, VMEM],
        out_specs=VMEM,
        scratch_shapes=[pltpu.VMEM((2, 8, shard_rows + half), f32)],
        compiler_params=params(),
        name="video_side",
    )(audio_count, video_range, video_query, kv_own, kv_out)

    z3, zm2 = from_z(row, 3), from_z(row, -2)
    z1, zm1 = from_z(row, 1), from_z(row, -1)
    z4, z2, zm3 = from_z(z3, 1), from_z(z3, -1), from_z(zm2, -1)
    audio_out = pl.pallas_call(
        assemble_kernel,
        out_shape=jax.ShapeDtypeStruct((ZS * XS * ABS, columns), bf16),
        in_specs=[VMEM] * 8,
        out_specs=ANY,
        scratch_shapes=[pltpu.SemaphoreType.DMA((ZS * XS,))],
        compiler_params=params(),
        name="assemble",
    )(row, z3, zm2, z1, zm1, z4, z2, zm3)
    return (video_out, audio_out)


def solution(mesh):
    return jax.shard_map(
        local,
        mesh=mesh,
        in_specs=(
            P("video", "audio"),
            P(None, "video", "audio"),
            P(None, "audio", None),
            P("video"),
            P(),
            P(),
        ),
        out_specs=(P("video", "audio"), P(None, "audio")),
        check_vma=False,
    )
```

```python
import math

import jax
import jax.numpy as jnp
from jax import lax
from jax.experimental import pallas as pl
from jax.experimental.pallas import tpu as pltpu
from jax.sharding import PartitionSpec as P

HEADS = 24
VBS = 256
ABS = 64
REACH = 2
ZS = 8
XS = 4
NEG = -1e30
LOG2E = 1.4426950408889634
BOTH = ("video", "audio")

VMEM = pl.BlockSpec(memory_space=pltpu.VMEM)
SMEM = pl.BlockSpec(memory_space=pltpu.SMEM)
ANY = pl.BlockSpec(memory_space=pl.ANY)


def params():
    return pltpu.CompilerParams(vmem_limit_bytes=24 * 1024 * 1024)


def place():
    v = lax.axis_index("video")
    return v, v // XS, v % XS


def sender_row(z, shard):
    ahead = lax.rem(z - shard + ZS, ZS)
    turn = jnp.where(ahead == 0, 2, jnp.where(ahead == 1, 1, jnp.where(ahead == ZS - 1, 3, 0)))
    return lax.rem(shard // 2 + turn, 4)


def line_of_sender(z, turn):
    return z + (2 if z % 2 else -2, 1, 0, -1)[turn]


def pack_kernel(src, out0, out1, sems):
    _, z, x = place()
    parts, _, columns = out0.shape
    first = sender_row(z, lax.axis_index("audio")) * 2 * columns
    rows = pl.ds(pl.multiple_of(x * ABS, ABS), ABS)
    copies = []
    for core, out in enumerate((out0, out1)):
        cols = pl.ds(pl.multiple_of(first + core * columns, 128), columns)
        for i in range(parts):
            copies.append(
                pltpu.make_async_copy(
                    src.at[i, rows, cols], out.at[i], sems.at[core * parts + i]
                )
            )
    for c in copies:
        c.start()
    for c in copies:
        c.wait()


def slot_block(z, x, slot):
    return z * XS + lax.rem(x - slot + XS, XS)


def split3(value):
    hi = value.astype(jnp.bfloat16).astype(jnp.float32)
    rest = value - hi
    mid = rest.astype(jnp.bfloat16).astype(jnp.float32)
    return hi, mid, rest - mid


def audio_kernel(scale, count, ranges, kv, edge, *refs):
    slots, outs, (queries, bias) = refs[:XS], refs[XS : XS + 5], refs[XS + 5 :]
    v, z, x = place()
    blocks = ranges.shape[0]
    columns = edge.shape[2]
    heads = columns // 128
    lane = lax.broadcasted_iota(jnp.int32, (ABS, 2 * VBS), 1)
    for slot in range(5):
        offset = slot - REACH
        at = x + offset
        dst = pl.ds(slot * ABS, ABS)
        own = (at >= 0) & (at < XS)

        @pl.when(own)
        def _():
            queries[dst, :] = slots[-offset % XS][0]

        if offset:

            @pl.when(jnp.logical_not(own))
            def _():
                row = (-1 - at if offset < 0 else XS + 1 - at) * ABS
                queries[dst, :] = edge[0, pl.ds(pl.multiple_of(row, ABS), ABS), :]

        block = v + offset
        inside = (block >= 0) & (block < blocks)
        safe = jnp.clip(block, 0, blocks - 1)
        first, last = ranges[safe, 0], ranges[safe, 1]
        live = []
        for j in range(2):
            vb = v * 2 + j
            paired = inside & (first <= vb) & (vb < last)
            live.append(jnp.where(paired, count[j], 0))
        allowed = (lane < live[0]) | ((lane >= VBS) & (lane < VBS + live[1]))
        bias[dst, :] = jnp.where(allowed, 0.0, NEG)
    stat_lane = lax.broadcasted_iota(jnp.int32, (5 * ABS, 128), 1)
    stats = jnp.zeros((5 * ABS, 128), jnp.float32)
    for h in range(heads):
        cols = slice(h * 128, (h + 1) * 128)
        s = lax.dot_general(
            queries[:, cols], kv[0, :, cols], (((1,), (1,)), ((), ())),
            preferred_element_type=jnp.float32,
        )
        s = s + bias[...]
        peak = jnp.max(s, axis=1, keepdims=True)
        e = jnp.exp2((s - peak) * scale)
        total = jnp.sum(e, axis=1, keepdims=True)
        o = lax.dot_general(
            e.astype(jnp.bfloat16), kv[1, :, cols], (((1,), (0,)), ((), ())),
            preferred_element_type=jnp.float32,
        )
        for i, part in enumerate(split3(peak * scale) + split3(total)):
            stats = jnp.where(stat_lane == h * 6 + i, part, stats)
        for slot in range(5):
            outs[slot][:, cols] = o[slot * ABS : (slot + 1) * ABS].astype(jnp.bfloat16)
    for slot in range(5):
        outs[slot][:, columns:] = stats[slot * ABS : (slot + 1) * ABS].astype(jnp.bfloat16)


def merge_kernel(*refs):
    parts, out = refs[:-1], refs[-1]
    columns = out.shape[1]
    stats = [p[:, columns:].astype(jnp.float32) for p in parts]
    for h in range(columns // 128):
        cols = slice(h * 128, (h + 1) * 128)

        def stat(s, i):
            at = h * 6 + i
            return s[:, at : at + 1] + s[:, at + 1 : at + 2] + s[:, at + 2 : at + 3]

        peaks = [stat(s, 0) for s in stats]
        peak = peaks[0]
        for p in peaks[1:]:
            peak = jnp.maximum(peak, p)
        total, blend = 0.0, 0.0
        for s, p, part in zip(stats, peaks, parts):
            keep = jnp.exp2(p - peak)
            total = total + stat(s, 3) * keep
            blend = blend + part[:, cols].astype(jnp.float32) * keep
        out[:, cols] = (blend / total).astype(jnp.bfloat16)


def video_kernel(scale, audio_count, ranges, query, edge, *refs):
    slots, out, bias = refs[:XS], refs[XS], refs[XS + 1]
    v, z, x = place()
    blocks = ranges.shape[0]
    columns = query.shape[1]
    lane = lax.broadcasted_iota(jnp.int32, (8, ABS * 2), 1)
    held = [slot_block(z, x, at) for at in range(XS)]
    held += [z * XS + jnp.where(x < REACH, -1 - at, XS + 1 - at) for at in range(REACH)]
    for pair in range(len(held) // 2):
        for j in range(2):
            vb = v * 2 + j
            allowed = None
            for side in range(2):
                block = held[pair * 2 + side]
                inside = (block >= 0) & (block < blocks)
                safe = jnp.clip(block, 0, blocks - 1)
                paired = inside & (ranges[safe, 0] <= vb) & (vb < ranges[safe, 1])
                live = jnp.where(paired, audio_count[safe], 0)
                here = (lane >= side * ABS) & (lane < side * ABS + live)
                allowed = here if allowed is None else allowed | here
            bias[j, :, pair * 2 * ABS : (pair + 1) * 2 * ABS] = jnp.where(allowed, 0.0, NEG)
    for h in range(columns // 128):
        cols = slice(h * 128, (h + 1) * 128)
        k, values = [
            jnp.concatenate([slot[i, :, cols] for slot in slots] + [edge[i - 1, :, cols]], axis=0)
            for i in (1, 2)
        ]
        for j in range(2):
            rows = slice(j * VBS, (j + 1) * VBS)
            s = lax.dot_general(
                query[rows, cols], k, (((1,), (1,)), ((), ())),
                preferred_element_type=jnp.float32,
            )
            s = s + bias[j, 0:1, :]
            peak = jnp.max(s, axis=1, keepdims=True)
            e = jnp.exp2((s - peak) * scale)
            total = jnp.sum(e, axis=1, keepdims=True)
            o = lax.dot_general(
                e.astype(jnp.bfloat16), values, (((1,), (0,)), ((), ())),
                preferred_element_type=jnp.float32,
            )
            out[rows, cols] = (o / total).astype(jnp.bfloat16)


ZHELD = (0, 3, -2, 1, -1, 4, 2, -3)


def assemble_kernel(*refs):
    chunks, out, sems = refs[:8], refs[8], refs[9]
    _, z, x = place()
    copies = []
    for i, rel in enumerate(ZHELD):
        zz = lax.rem(z + rel + ZS, ZS)
        for k in range(XS):
            row = (zz * XS + lax.rem(x - k + XS, XS)) * ABS
            copies.append(
                pltpu.make_async_copy(
                    chunks[i].at[pl.ds(k * ABS, ABS), :],
                    out.at[pl.ds(pl.multiple_of(row, ABS), ABS), :],
                    sems.at[i * XS + k],
                )
            )
    for c in copies:
        c.start()
    for c in copies:
        c.wait()


def shifted(value, step):
    n = ZS * XS
    return lax.ppermute(value, "video", [(v, (v + step) % n) for v in range(n)])


def along_x(value, step):
    pairs = [(z * XS + x, z * XS + (x + step) % XS) for z in range(ZS) for x in range(XS)]
    return lax.ppermute(value, "video", pairs)


def from_z(value, rel):
    return shifted(value, -rel * XS)


def local(video_query, video_kv, audio_qkv, video_count, audio_count, video_range):
    seg_rows, columns = video_query.shape
    shard_rows = audio_qkv.shape[1]
    half = REACH * ABS
    bf16 = jnp.bfloat16
    f32 = jnp.float32
    scale = LOG2E / math.sqrt(128)
    audio_devices = lax.axis_size("audio")

    def flat(z, x, a):
        return ((z % ZS) * XS + x) * audio_devices + a

    pack0, pack1 = pl.pallas_call(
        pack_kernel,
        out_shape=(jax.ShapeDtypeStruct((3, ABS, columns), bf16),) * 2,
        in_specs=[ANY],
        out_specs=(VMEM,) * 2,
        scratch_shapes=[pltpu.SemaphoreType.DMA((6,))],
        compiler_params=pltpu.CompilerParams(vmem_limit_bytes=60 * 1024 * 1024),
        name="pack",
    )(audio_qkv)

    def to_core(value, core):
        pairs = []
        for z in range(ZS):
            for xx in range(XS):
                for y in range(audio_devices // 2):
                    sender = line_of_sender(z, (y - z // 2) % 4)
                    pairs.append((flat(sender, xx, z), flat(z, xx, 2 * y + core)))
        return lax.ppermute(value, BOTH, pairs)

    def between_lines(value, step):
        n = ZS * XS
        pairs = [(v, (v + step if v % XS < REACH else v - step) % n) for v in range(n)]
        return lax.ppermute(value, "video", pairs)

    own = to_core(pack0, 0) + to_core(pack1, 1)
    slots = [own] + [along_x(own, k) for k in range(1, XS)]

    odd = lax.axis_index("video") % 2 == 1
    near = [jnp.where(odd, slots[at + 2], slots[at + 1]) for at in range(REACH)]
    near = jnp.concatenate(near, axis=1)
    edge, near_kv = lax.optimization_barrier((between_lines(near[:1], XS), near[1:]))
    edge_kv = between_lines(near_kv, XS)
    parts = pl.pallas_call(
        lambda *refs: audio_kernel(scale, *refs),
        out_shape=(jax.ShapeDtypeStruct((ABS, columns + 128), bf16),) * 5,
        in_specs=[SMEM] * 2 + [VMEM] * (2 + XS),
        out_specs=(VMEM,) * 5,
        scratch_shapes=[
            pltpu.VMEM((5 * ABS, columns), bf16),
            pltpu.VMEM((5 * ABS, seg_rows), f32),
        ],
        compiler_params=params(),
        name="audio_side",
    )(video_count, video_range, video_kv, edge, *slots)
    held = [
        shifted(part, slot - REACH) if slot != REACH else part for slot, part in enumerate(parts)
    ]
    block_out = pl.pallas_call(
        merge_kernel,
        out_shape=jax.ShapeDtypeStruct((ABS, columns), bf16),
        in_specs=[VMEM] * 5,
        out_specs=VMEM,
        compiler_params=params(),
        name="merge",
    )(*held)

    row = jnp.concatenate([block_out] + [along_x(block_out, k) for k in range(1, XS)], axis=0)
    row, edge_kv = lax.optimization_barrier((row, edge_kv))
    video_out = pl.pallas_call(
        lambda *refs: video_kernel(scale, *refs),
        out_shape=jax.ShapeDtypeStruct((seg_rows, columns), bf16),
        in_specs=[SMEM, SMEM] + [VMEM] * (2 + XS),
        out_specs=VMEM,
        scratch_shapes=[pltpu.VMEM((2, 8, shard_rows + half), f32)],
        compiler_params=params(),
        name="video_side",
    )(audio_count, video_range, video_query, edge_kv, *slots)

    z3, zm2 = from_z(row, 3), from_z(row, -2)
    z1, zm1 = from_z(row, 1), from_z(row, -1)
    z4, z2, zm3 = from_z(z3, 1), from_z(z3, -1), from_z(zm2, -1)
    audio_out = pl.pallas_call(
        assemble_kernel,
        out_shape=jax.ShapeDtypeStruct((ZS * XS * ABS, columns), bf16),
        in_specs=[VMEM] * 8,
        out_specs=ANY,
        scratch_shapes=[pltpu.SemaphoreType.DMA((ZS * XS,))],
        compiler_params=params(),
        name="assemble",
    )(row, z3, zm2, z1, zm1, z4, z2, zm3)
    return (video_out, audio_out)


def solution(mesh):
    return jax.shard_map(
        local,
        mesh=mesh,
        in_specs=(
            P("video", "audio"),
            P(None, "video", "audio"),
            P(None, "audio", None),
            P("video"),
            P(),
            P(),
        ),
        out_specs=(P("video", "audio"), P(None, "audio")),
        check_vma=False,
    )
```

```python
import math

import jax
import jax.numpy as jnp
from jax import lax
from jax.experimental import pallas as pl
from jax.experimental.pallas import tpu as pltpu
from jax.sharding import PartitionSpec as P

HEADS = 24
VBS = 256
ABS = 64
REACH = 2
ZS = 8
XS = 4
NEG = -1e30
LOG2E = 1.4426950408889634
BOTH = ("video", "audio")

VMEM = pl.BlockSpec(memory_space=pltpu.VMEM)
SMEM = pl.BlockSpec(memory_space=pltpu.SMEM)
ANY = pl.BlockSpec(memory_space=pl.ANY)


def params():
    return pltpu.CompilerParams(vmem_limit_bytes=24 * 1024 * 1024)


def place():
    v = lax.axis_index("video")
    return v, v // XS, v % XS


def sender_row(z, shard):
    ahead = lax.rem(z - shard + ZS, ZS)
    turn = jnp.where(ahead == 0, 2, jnp.where(ahead == 1, 1, jnp.where(ahead == ZS - 1, 3, 0)))
    return lax.rem(shard // 2 + turn, 4)


def line_of_sender(z, turn):
    return z + (2 if z % 2 else -2, 1, 0, -1)[turn]


def pack_kernel(src, out0, out1, sems):
    _, z, x = place()
    parts, _, columns = out0.shape
    first = sender_row(z, lax.axis_index("audio")) * 2 * columns
    rows = pl.ds(pl.multiple_of(x * ABS, ABS), ABS)
    copies = []
    for core, out in enumerate((out0, out1)):
        cols = pl.ds(pl.multiple_of(first + core * columns, 128), columns)
        for i in range(parts):
            copies.append(
                pltpu.make_async_copy(
                    src.at[i, rows, cols], out.at[i], sems.at[core * parts + i]
                )
            )
    for c in copies:
        c.start()
    for c in copies:
        c.wait()


def slot_block(z, x, slot):
    return z * XS + lax.rem(x - slot + XS, XS)


def split3(value):
    hi = value.astype(jnp.bfloat16).astype(jnp.float32)
    rest = value - hi
    mid = rest.astype(jnp.bfloat16).astype(jnp.float32)
    return hi, mid, rest - mid


def audio_kernel(scale, count, ranges, kv, edge, *refs):
    slots, outs, (queries, bias) = refs[:XS], refs[XS : XS + 5], refs[XS + 5 :]
    v, z, x = place()
    blocks = ranges.shape[0]
    columns = edge.shape[2]
    heads = columns // 128
    lane = lax.broadcasted_iota(jnp.int32, (ABS, 2 * VBS), 1)
    for slot in range(5):
        offset = slot - REACH
        at = x + offset
        dst = pl.ds(slot * ABS, ABS)
        own = (at >= 0) & (at < XS)

        @pl.when(own)
        def _():
            queries[dst, :] = slots[-offset % XS][0]

        if offset:

            @pl.when(jnp.logical_not(own))
            def _():
                row = (-1 - at if offset < 0 else XS + 1 - at) * ABS
                queries[dst, :] = edge[0, pl.ds(pl.multiple_of(row, ABS), ABS), :]

        block = v + offset
        inside = (block >= 0) & (block < blocks)
        safe = jnp.clip(block, 0, blocks - 1)
        first, last = ranges[safe, 0], ranges[safe, 1]
        live = []
        for j in range(2):
            vb = v * 2 + j
            paired = inside & (first <= vb) & (vb < last)
            live.append(jnp.where(paired, count[j], 0))
        allowed = (lane < live[0]) | ((lane >= VBS) & (lane < VBS + live[1]))
        bias[dst, :] = jnp.where(allowed, 0.0, NEG)
    stat_lane = lax.broadcasted_iota(jnp.int32, (5 * ABS, 128), 1)
    stats = jnp.zeros((5 * ABS, 128), jnp.float32)
    for h in range(heads):
        cols = slice(h * 128, (h + 1) * 128)
        s = lax.dot_general(
            queries[:, cols], kv[0, :, cols], (((1,), (1,)), ((), ())),
            preferred_element_type=jnp.float32,
        )
        s = s + bias[...]
        peak = jnp.max(s, axis=1, keepdims=True)
        e = jnp.exp2((s - peak) * scale)
        total = jnp.sum(e, axis=1, keepdims=True)
        o = lax.dot_general(
            e.astype(jnp.bfloat16), kv[1, :, cols], (((1,), (0,)), ((), ())),
            preferred_element_type=jnp.float32,
        )
        for i, part in enumerate(split3(peak * scale) + split3(total)):
            stats = jnp.where(stat_lane == h * 6 + i, part, stats)
        for slot in range(5):
            outs[slot][:, cols] = o[slot * ABS : (slot + 1) * ABS].astype(jnp.bfloat16)
    for slot in range(5):
        outs[slot][:, columns:] = stats[slot * ABS : (slot + 1) * ABS].astype(jnp.bfloat16)


def merge_kernel(*refs):
    parts, out = refs[:-1], refs[-1]
    columns = out.shape[1]
    stats = [p[:, columns:].astype(jnp.float32) for p in parts]
    for h in range(columns // 128):
        cols = slice(h * 128, (h + 1) * 128)

        def stat(s, i):
            at = h * 6 + i
            return s[:, at : at + 1] + s[:, at + 1 : at + 2] + s[:, at + 2 : at + 3]

        peaks = [stat(s, 0) for s in stats]
        peak = peaks[0]
        for p in peaks[1:]:
            peak = jnp.maximum(peak, p)
        total, blend = 0.0, 0.0
        for s, p, part in zip(stats, peaks, parts):
            keep = jnp.exp2(p - peak)
            total = total + stat(s, 3) * keep
            blend = blend + part[:, cols].astype(jnp.float32) * keep
        out[:, cols] = (blend / total).astype(jnp.bfloat16)


def video_kernel(scale, audio_count, ranges, query, edge, *refs):
    slots, out, bias = refs[:XS], refs[XS], refs[XS + 1]
    v, z, x = place()
    blocks = ranges.shape[0]
    columns = query.shape[1]
    lane = lax.broadcasted_iota(jnp.int32, (8, ABS * 2), 1)
    held = [slot_block(z, x, at) for at in range(XS)]
    held += [z * XS + jnp.where(x < REACH, -1 - at, XS + 1 - at) for at in range(REACH)]
    for pair in range(len(held) // 2):
        for j in range(2):
            vb = v * 2 + j
            allowed = None
            for side in range(2):
                block = held[pair * 2 + side]
                inside = (block >= 0) & (block < blocks)
                safe = jnp.clip(block, 0, blocks - 1)
                paired = inside & (ranges[safe, 0] <= vb) & (vb < ranges[safe, 1])
                live = jnp.where(paired, audio_count[safe], 0)
                here = (lane >= side * ABS) & (lane < side * ABS + live)
                allowed = here if allowed is None else allowed | here
            bias[j, :, pair * 2 * ABS : (pair + 1) * 2 * ABS] = jnp.where(allowed, 0.0, NEG)
    for h in range(columns // 128):
        cols = slice(h * 128, (h + 1) * 128)
        k, values = [
            jnp.concatenate([slot[i, :, cols] for slot in slots] + [edge[i - 1, :, cols]], axis=0)
            for i in (1, 2)
        ]
        for j in range(2):
            rows = slice(j * VBS, (j + 1) * VBS)
            s = lax.dot_general(
                query[rows, cols], k, (((1,), (1,)), ((), ())),
                preferred_element_type=jnp.float32,
            )
            s = s + bias[j, 0:1, :]
            peak = jnp.max(s, axis=1, keepdims=True)
            e = jnp.exp2((s - peak) * scale)
            total = jnp.sum(e, axis=1, keepdims=True)
            o = lax.dot_general(
                e.astype(jnp.bfloat16), values, (((1,), (0,)), ((), ())),
                preferred_element_type=jnp.float32,
            )
            out[rows, cols] = (o / total).astype(jnp.bfloat16)


def assemble_kernel(held, *refs):
    chunks, (out, sems) = refs[: len(held)], refs[-2:]
    _, z, x = place()
    copies = []
    for i, rel in enumerate(held):
        zz = lax.rem(z + rel + ZS, ZS)
        for k in range(XS):
            row = (zz * XS + lax.rem(x - k + XS, XS)) * ABS
            copies.append(
                pltpu.make_async_copy(
                    chunks[i].at[pl.ds(k * ABS, ABS), :],
                    out.at[pl.ds(pl.multiple_of(row, ABS), ABS), :],
                    sems.at[i * XS + k],
                )
            )
    for c in copies:
        c.start()
    for c in copies:
        c.wait()


def shifted(value, step):
    n = ZS * XS
    return lax.ppermute(value, "video", [(v, (v + step) % n) for v in range(n)])


def along_x(value, step):
    pairs = [(z * XS + x, z * XS + (x + step) % XS) for z in range(ZS) for x in range(XS)]
    return lax.ppermute(value, "video", pairs)


def from_z(value, rel):
    return shifted(value, -rel * XS)


def local(video_query, video_kv, audio_qkv, video_count, audio_count, video_range):
    seg_rows, columns = video_query.shape
    shard_rows = audio_qkv.shape[1]
    half = REACH * ABS
    bf16 = jnp.bfloat16
    f32 = jnp.float32
    scale = LOG2E / math.sqrt(128)
    audio_devices = lax.axis_size("audio")

    def flat(z, x, a):
        return ((z % ZS) * XS + x) * audio_devices + a

    pack0, pack1 = pl.pallas_call(
        pack_kernel,
        out_shape=(jax.ShapeDtypeStruct((3, ABS, columns), bf16),) * 2,
        in_specs=[ANY],
        out_specs=(VMEM,) * 2,
        scratch_shapes=[pltpu.SemaphoreType.DMA((6,))],
        compiler_params=pltpu.CompilerParams(vmem_limit_bytes=60 * 1024 * 1024),
        name="pack",
    )(audio_qkv)

    def to_core(value, core):
        pairs = []
        for z in range(ZS):
            for xx in range(XS):
                for y in range(audio_devices // 2):
                    sender = line_of_sender(z, (y - z // 2) % 4)
                    pairs.append((flat(sender, xx, z), flat(z, xx, 2 * y + core)))
        return lax.ppermute(value, BOTH, pairs)

    def between_lines(value, step):
        n = ZS * XS
        pairs = [(v, (v + step if v % XS < REACH else v - step) % n) for v in range(n)]
        return lax.ppermute(value, "video", pairs)

    own = to_core(pack0, 0) + to_core(pack1, 1)
    slots = [own] + [along_x(own, k) for k in range(1, XS)]

    odd = lax.axis_index("video") % 2 == 1
    near = [jnp.where(odd, slots[at + 2], slots[at + 1]) for at in range(REACH)]
    near = jnp.concatenate(near, axis=1)
    edge, near_kv = lax.optimization_barrier((between_lines(near[:1], XS), near[1:]))
    edge_kv = between_lines(near_kv, XS)
    parts = pl.pallas_call(
        lambda *refs: audio_kernel(scale, *refs),
        out_shape=(jax.ShapeDtypeStruct((ABS, columns + 128), bf16),) * 5,
        in_specs=[SMEM] * 2 + [VMEM] * (2 + XS),
        out_specs=(VMEM,) * 5,
        scratch_shapes=[
            pltpu.VMEM((5 * ABS, columns), bf16),
            pltpu.VMEM((5 * ABS, seg_rows), f32),
        ],
        compiler_params=params(),
        name="audio_side",
    )(video_count, video_range, video_kv, edge, *slots)
    held = [
        shifted(part, slot - REACH) if slot != REACH else part for slot, part in enumerate(parts)
    ]
    block_out = pl.pallas_call(
        merge_kernel,
        out_shape=jax.ShapeDtypeStruct((ABS, columns), bf16),
        in_specs=[VMEM] * 5,
        out_specs=VMEM,
        compiler_params=params(),
        name="merge",
    )(*held)

    row = jnp.concatenate([block_out] + [along_x(block_out, k) for k in range(1, XS)], axis=0)
    row, edge_kv = lax.optimization_barrier((row, edge_kv))
    video_out = pl.pallas_call(
        lambda *refs: video_kernel(scale, *refs),
        out_shape=jax.ShapeDtypeStruct((seg_rows, columns), bf16),
        in_specs=[SMEM, SMEM] + [VMEM] * (2 + XS),
        out_specs=VMEM,
        scratch_shapes=[pltpu.VMEM((2, 8, shard_rows + half), f32)],
        compiler_params=params(),
        name="video_side",
    )(audio_count, video_range, video_query, edge_kv, *slots)

    z3, zm2 = from_z(row, 3), from_z(row, -2)
    z1, zm1 = from_z(row, 1), from_z(row, -1)
    z3, video_out = lax.optimization_barrier((z3, video_out))
    z4, z2, zm3 = from_z(z3, 1), from_z(z3, -1), from_z(zm2, -1)
    whole = jax.ShapeDtypeStruct((ZS * XS * ABS, columns), bf16)

    def assembled(held, chunks, *before):
        n = len(chunks)
        return pl.pallas_call(
            lambda *refs: assemble_kernel(held, *refs),
            out_shape=whole,
            in_specs=[VMEM] * n + [ANY] * len(before),
            out_specs=ANY,
            scratch_shapes=[pltpu.SemaphoreType.DMA((n * XS,))],
            input_output_aliases={n: 0} if before else {},
            compiler_params=params(),
            name="assemble",
        )(*chunks, *before)

    early = assembled((0, 3, -2, 1, -1), (row, z3, zm2, z1, zm1))
    audio_out = assembled((4, 2, -3), (z4, z2, zm3), early)
    return (video_out, audio_out)


def solution(mesh):
    return jax.shard_map(
        local,
        mesh=mesh,
        in_specs=(
            P("video", "audio"),
            P(None, "video", "audio"),
            P(None, "audio", None),
            P("video"),
            P(),
            P(),
        ),
        out_specs=(P("video", "audio"), P(None, "audio")),
        check_vma=False,
    )
```

```python
import math

import jax
import jax.numpy as jnp
from jax import lax
from jax.experimental import pallas as pl
from jax.experimental.pallas import tpu as pltpu
from jax.sharding import PartitionSpec as P

HEADS = 24
VBS = 256
ABS = 64
REACH = 2
ZS = 8
XS = 4
NEG = -1e30
LOG2E = 1.4426950408889634
BOTH = ("video", "audio")

VMEM = pl.BlockSpec(memory_space=pltpu.VMEM)
SMEM = pl.BlockSpec(memory_space=pltpu.SMEM)
ANY = pl.BlockSpec(memory_space=pl.ANY)


def params():
    return pltpu.CompilerParams(vmem_limit_bytes=24 * 1024 * 1024)


def place():
    v = lax.axis_index("video")
    return v, v // XS, v % XS


def sender_row(z, shard):
    ahead = lax.rem(z - shard + ZS, ZS)
    turn = jnp.where(ahead == 0, 2, jnp.where(ahead == 1, 1, jnp.where(ahead == ZS - 1, 3, 0)))
    return lax.rem(shard // 2 + turn, 4)


def line_of_sender(z, turn):
    return z + (2 if z % 2 else -2, 1, 0, -1)[turn]


def pack_kernel(src, out0, out1, sems):
    _, z, x = place()
    parts, _, columns = out0.shape
    first = sender_row(z, lax.axis_index("audio")) * 2 * columns
    rows = pl.ds(pl.multiple_of(x * ABS, ABS), ABS)
    copies = []
    for core, out in enumerate((out0, out1)):
        cols = pl.ds(pl.multiple_of(first + core * columns, 128), columns)
        for i in range(parts):
            copies.append(
                pltpu.make_async_copy(
                    src.at[i, rows, cols], out.at[i], sems.at[core * parts + i]
                )
            )
    for c in copies:
        c.start()
    for c in copies:
        c.wait()


def slot_block(z, x, slot):
    return z * XS + lax.rem(x - slot + XS, XS)


def split3(value):
    hi = value.astype(jnp.bfloat16).astype(jnp.float32)
    rest = value - hi
    mid = rest.astype(jnp.bfloat16).astype(jnp.float32)
    return hi, mid, rest - mid


def audio_kernel(scale, count, ranges, kv, edge, *refs):
    slots, outs, (queries, bias) = refs[:XS], refs[XS : XS + 5], refs[XS + 5 :]
    v, z, x = place()
    blocks = ranges.shape[0]
    columns = edge.shape[2]
    heads = columns // 128
    lane = lax.broadcasted_iota(jnp.int32, (ABS, 2 * VBS), 1)
    for slot in range(5):
        offset = slot - REACH
        at = x + offset
        dst = pl.ds(slot * ABS, ABS)
        own = (at >= 0) & (at < XS)

        @pl.when(own)
        def _():
            queries[dst, :] = slots[-offset % XS][0]

        if offset:

            @pl.when(jnp.logical_not(own))
            def _():
                row = (-1 - at if offset < 0 else XS + 1 - at) * ABS
                queries[dst, :] = edge[0, pl.ds(pl.multiple_of(row, ABS), ABS), :]

        block = v + offset
        inside = (block >= 0) & (block < blocks)
        safe = jnp.clip(block, 0, blocks - 1)
        first, last = ranges[safe, 0], ranges[safe, 1]
        live = []
        for j in range(2):
            vb = v * 2 + j
            paired = inside & (first <= vb) & (vb < last)
            live.append(jnp.where(paired, count[j], 0))
        allowed = (lane < live[0]) | ((lane >= VBS) & (lane < VBS + live[1]))
        bias[dst, :] = jnp.where(allowed, 0.0, NEG)
    stat_lane = lax.broadcasted_iota(jnp.int32, (5 * ABS, 128), 1)
    stats = jnp.zeros((5 * ABS, 128), jnp.float32)
    for h in range(heads):
        cols = slice(h * 128, (h + 1) * 128)
        s = lax.dot_general(
            queries[:, cols], kv[0, :, cols], (((1,), (1,)), ((), ())),
            preferred_element_type=jnp.float32,
        )
        s = s + bias[...]
        peak = jnp.max(s, axis=1, keepdims=True)
        e = jnp.exp2((s - peak) * scale)
        total = jnp.sum(e, axis=1, keepdims=True)
        o = lax.dot_general(
            e.astype(jnp.bfloat16), kv[1, :, cols], (((1,), (0,)), ((), ())),
            preferred_element_type=jnp.float32,
        )
        for i, part in enumerate(split3(peak * scale) + split3(total)):
            stats = jnp.where(stat_lane == h * 6 + i, part, stats)
        for slot in range(5):
            outs[slot][:, cols] = o[slot * ABS : (slot + 1) * ABS].astype(jnp.bfloat16)
    for slot in range(5):
        outs[slot][:, columns:] = stats[slot * ABS : (slot + 1) * ABS].astype(jnp.bfloat16)


def merge_kernel(*refs):
    parts, out = refs[:-1], refs[-1]
    columns = out.shape[1]
    stats = [p[:, columns:].astype(jnp.float32) for p in parts]
    for h in range(columns // 128):
        cols = slice(h * 128, (h + 1) * 128)

        def stat(s, i):
            at = h * 6 + i
            return s[:, at : at + 1] + s[:, at + 1 : at + 2] + s[:, at + 2 : at + 3]

        peaks = [stat(s, 0) for s in stats]
        peak = peaks[0]
        for p in peaks[1:]:
            peak = jnp.maximum(peak, p)
        total, blend = 0.0, 0.0
        for s, p, part in zip(stats, peaks, parts):
            keep = jnp.exp2(p - peak)
            total = total + stat(s, 3) * keep
            blend = blend + part[:, cols].astype(jnp.float32) * keep
        out[:, cols] = (blend / total).astype(jnp.bfloat16)


def video_kernel(scale, audio_count, ranges, query, edge, *refs):
    slots, out, bias = refs[:XS], refs[XS], refs[XS + 1]
    v, z, x = place()
    blocks = ranges.shape[0]
    columns = query.shape[1]
    lane = lax.broadcasted_iota(jnp.int32, (8, ABS * 2), 1)
    held = [slot_block(z, x, at) for at in range(XS)]
    held += [z * XS + jnp.where(x < REACH, -1 - at, XS + 1 - at) for at in range(REACH)]
    for pair in range(len(held) // 2):
        for j in range(2):
            vb = v * 2 + j
            allowed = None
            for side in range(2):
                block = held[pair * 2 + side]
                inside = (block >= 0) & (block < blocks)
                safe = jnp.clip(block, 0, blocks - 1)
                paired = inside & (ranges[safe, 0] <= vb) & (vb < ranges[safe, 1])
                live = jnp.where(paired, audio_count[safe], 0)
                here = (lane >= side * ABS) & (lane < side * ABS + live)
                allowed = here if allowed is None else allowed | here
            bias[j, :, pair * 2 * ABS : (pair + 1) * 2 * ABS] = jnp.where(allowed, 0.0, NEG)
    for h in range(columns // 128):
        cols = slice(h * 128, (h + 1) * 128)
        k, values = [
            jnp.concatenate([slot[i, :, cols] for slot in slots] + [edge[i - 1, :, cols]], axis=0)
            for i in (1, 2)
        ]
        for j in range(2):
            rows = slice(j * VBS, (j + 1) * VBS)
            s = lax.dot_general(
                query[rows, cols], k, (((1,), (1,)), ((), ())),
                preferred_element_type=jnp.float32,
            )
            s = s + bias[j, 0:1, :]
            peak = jnp.max(s, axis=1, keepdims=True)
            e = jnp.exp2((s - peak) * scale)
            total = jnp.sum(e, axis=1, keepdims=True)
            o = lax.dot_general(
                e.astype(jnp.bfloat16), values, (((1,), (0,)), ((), ())),
                preferred_element_type=jnp.float32,
            )
            out[rows, cols] = (o / total).astype(jnp.bfloat16)


def assemble_kernel(held, *refs):
    chunks, (out, sems) = refs[: len(held)], refs[-2:]
    _, z, x = place()
    copies = []
    for i, rel in enumerate(held):
        zz = lax.rem(z + rel + ZS, ZS)
        for k in range(XS):
            row = (zz * XS + lax.rem(x - k + XS, XS)) * ABS
            copies.append(
                pltpu.make_async_copy(
                    chunks[i].at[pl.ds(k * ABS, ABS), :],
                    out.at[pl.ds(pl.multiple_of(row, ABS), ABS), :],
                    sems.at[i * XS + k],
                )
            )
    for c in copies:
        c.start()
    for c in copies:
        c.wait()


def shifted(value, step):
    n = ZS * XS
    return lax.ppermute(value, "video", [(v, (v + step) % n) for v in range(n)])


def along_x(value, step):
    pairs = [(z * XS + x, z * XS + (x + step) % XS) for z in range(ZS) for x in range(XS)]
    return lax.ppermute(value, "video", pairs)


def from_z(value, rel):
    return shifted(value, -rel * XS)


def local(video_query, video_kv, audio_qkv, video_count, audio_count, video_range):
    seg_rows, columns = video_query.shape
    shard_rows = audio_qkv.shape[1]
    half = REACH * ABS
    bf16 = jnp.bfloat16
    f32 = jnp.float32
    scale = LOG2E / math.sqrt(128)
    audio_devices = lax.axis_size("audio")

    def flat(z, x, a):
        return ((z % ZS) * XS + x) * audio_devices + a

    pack0, pack1 = pl.pallas_call(
        pack_kernel,
        out_shape=(jax.ShapeDtypeStruct((3, ABS, columns), bf16),) * 2,
        in_specs=[ANY],
        out_specs=(VMEM,) * 2,
        scratch_shapes=[pltpu.SemaphoreType.DMA((6,))],
        compiler_params=pltpu.CompilerParams(vmem_limit_bytes=60 * 1024 * 1024),
        name="pack",
    )(audio_qkv)

    def to_core(value, core):
        pairs = []
        for z in range(ZS):
            for xx in range(XS):
                for y in range(audio_devices // 2):
                    sender = line_of_sender(z, (y - z // 2) % 4)
                    pairs.append((flat(sender, xx, z), flat(z, xx, 2 * y + core)))
        return lax.ppermute(value, BOTH, pairs)

    def between_lines(value, step):
        n = ZS * XS
        pairs = [(v, (v + step if v % XS < REACH else v - step) % n) for v in range(n)]
        return lax.ppermute(value, "video", pairs)

    own = to_core(pack0, 0) + to_core(pack1, 1)
    slots = [own] + [along_x(own, k) for k in range(1, XS)]

    odd = lax.axis_index("video") % 2 == 1

    def near(held):
        pairs = [jnp.where(odd, held[at + 2], held[at + 1]) for at in range(REACH)]
        return between_lines(jnp.concatenate(pairs, axis=1), XS)

    edge, *later_kv = lax.optimization_barrier(
        (near([slot[:1] for slot in slots]), *[slot[1:] for slot in slots])
    )
    edge_kv = near(later_kv)
    parts = pl.pallas_call(
        lambda *refs: audio_kernel(scale, *refs),
        out_shape=(jax.ShapeDtypeStruct((ABS, columns + 128), bf16),) * 5,
        in_specs=[SMEM] * 2 + [VMEM] * (2 + XS),
        out_specs=(VMEM,) * 5,
        scratch_shapes=[
            pltpu.VMEM((5 * ABS, columns), bf16),
            pltpu.VMEM((5 * ABS, seg_rows), f32),
        ],
        compiler_params=params(),
        name="audio_side",
    )(video_count, video_range, video_kv, edge, *slots)
    held = [
        shifted(part, slot - REACH) if slot != REACH else part for slot, part in enumerate(parts)
    ]
    block_out = pl.pallas_call(
        merge_kernel,
        out_shape=jax.ShapeDtypeStruct((ABS, columns), bf16),
        in_specs=[VMEM] * 5,
        out_specs=VMEM,
        compiler_params=params(),
        name="merge",
    )(*held)

    row = jnp.concatenate([block_out] + [along_x(block_out, k) for k in range(1, XS)], axis=0)
    row, edge_kv = lax.optimization_barrier((row, edge_kv))
    video_out = pl.pallas_call(
        lambda *refs: video_kernel(scale, *refs),
        out_shape=jax.ShapeDtypeStruct((seg_rows, columns), bf16),
        in_specs=[SMEM, SMEM] + [VMEM] * (2 + XS),
        out_specs=VMEM,
        scratch_shapes=[pltpu.VMEM((2, 8, shard_rows + half), f32)],
        compiler_params=params(),
        name="video_side",
    )(audio_count, video_range, video_query, edge_kv, *slots)

    z3, zm2 = from_z(row, 3), from_z(row, -2)
    z1, zm1 = from_z(row, 1), from_z(row, -1)
    z3, video_out = lax.optimization_barrier((z3, video_out))
    z4, z2, zm3 = from_z(z3, 1), from_z(z3, -1), from_z(zm2, -1)
    whole = jax.ShapeDtypeStruct((ZS * XS * ABS, columns), bf16)

    def assembled(held, chunks, *before):
        n = len(chunks)
        return pl.pallas_call(
            lambda *refs: assemble_kernel(held, *refs),
            out_shape=whole,
            in_specs=[VMEM] * n + [ANY] * len(before),
            out_specs=ANY,
            scratch_shapes=[pltpu.SemaphoreType.DMA((n * XS,))],
            input_output_aliases={n: 0} if before else {},
            compiler_params=params(),
            name="assemble",
        )(*chunks, *before)

    early = assembled((0, 3, -2, 1, -1), (row, z3, zm2, z1, zm1))
    audio_out = assembled((4, 2, -3), (z4, z2, zm3), early)
    return (video_out, audio_out)


def solution(mesh):
    return jax.shard_map(
        local,
        mesh=mesh,
        in_specs=(
            P("video", "audio"),
            P(None, "video", "audio"),
            P(None, "audio", None),
            P("video"),
            P(),
            P(),
        ),
        out_specs=(P("video", "audio"), P(None, "audio")),
        check_vma=False,
    )
```
